32 devices in a mesh: groups: 1, ep: 16 (over z, y, x), side: 2 (over core).
Axes of the slice: x: 2, y: 2, z: 4, core: 2. Of those that a mesh axis runs over, the one named last changes fastest.
Arguments:
- queries: bfloat16 [128, 128, 576], P(('groups', 'ep', 'side')), may hold values from -16 to 16
- latent_cache: bfloat16 [64, 128, 576], P(('groups', 'ep', 'side')), may hold values from -16 to 16
- new_latent: bfloat16 [128, 576], P(('groups', 'ep', 'side')), may hold values from -6 to 6
- lengths: int32 [64], P(('groups', 'ep', 'side')), may hold values from 2 to 128
- residual: bfloat16 [128, 3584], P(('groups', 'ep', 'side')), may hold values from -6 to 6
- norm_gain: float32 [3584], replicated, may hold values from 0.5 to 1.5
- value_up: bfloat16 [128, 512, 128], P(('ep', 'side')), may hold values from -0.25 to 0.25
- output_proj: bfloat16 [128, 128, 3584], P(('ep', 'side')), may hold values from -0.1875 to 0.1875
- expert_ids: int32 [128, 8], P(('groups', 'ep', 'side')), may hold values from 0 to 15, all different within a row; in each aligned block of 4 rows (0 to 3, 4 to 7, ...) at most 2 rows name the same one
- expert_weights: float32 [128, 8], P(('groups', 'ep', 'side')), may hold values from 0.05 to 0.4
- gate_proj: bfloat16 [16, 3584, 1024], P('ep', None, 'side'), may hold values from -0.09375 to 0.09375
- up_proj: bfloat16 [16, 3584, 1024], P('ep', None, 'side'), may hold values from -0.09375 to 0.09375
- down_proj: bfloat16 [16, 1024, 3584], P('ep', 'side'), may hold values from -0.1875 to 0.1875
Outputs:
- layer_out: bfloat16 [128, 3584], P(('groups', 'ep', 'side'))
The draws below stay inside these ranges and needn't reach their ends.
Inputs may be any that keep to these rules, and one draw needn't show every extreme that they name: `expert_ids`: each row names 8 different experts. The 4 rows of one device name any one expert at most 2 times, and in every draw some device's rows name some expert exactly 2 times.
All inputs are finite; a program needn't handle non-finite values.
Results may differ from the reference program's by a relative error of at most 0.0056.
Values may be sent and summed in bfloat16 or wider, within the bound.
A program may use at most 64 MiB of HBM per device.

```python
import math
import jax
import jax.numpy as jnp
import numpy as np
from jax import lax

H = 128
LAT = 512
VH = 128
QKD = 192
D = 3584
FF = 1024
TOP = 8
STEPS = 2
CTX = 128
KD = 576
EXPERTS = 16
TOK_PD = 4
REQS = 64
TOKENS = 128
CAP = 2
N_SIDE = 2


def draw_queries(key, part):
    drawn = jnp.clip(jax.random.normal(jax.random.fold_in(key, 11), (TOKENS, H, KD), jnp.float32), -6.0, 6.0)
    return drawn.astype(jnp.bfloat16)


def draw_latent_cache(key, part):
    drawn = jnp.clip(jax.random.normal(jax.random.fold_in(key, 21), (REQS, CTX, KD), jnp.float32), -6.0, 6.0)
    return drawn.astype(jnp.bfloat16)


def place_ends(values, key, smallest, top_value):
    spot = [jax.random.randint(jax.random.fold_in(key, axis), (), 0, length) for axis, length in enumerate(values.shape)]
    main_axis = values.shape.index(max(values.shape))
    neighbour = spot[:main_axis] + [(spot[main_axis] + 1) % values.shape[main_axis]] + spot[main_axis + 1:]
    return values.at[tuple(spot)].set(smallest).at[tuple(neighbour)].set(top_value)


def block_levels(rng, extent, pieces, low, top_value):
    def one(axis_at, blocks):
        heights = jax.random.uniform(jax.random.fold_in(jax.random.fold_in(rng, 6), axis_at), (blocks,), jnp.float32, low / len(pieces), top_value / len(pieces))
        return jnp.repeat(jnp.exp(heights), extent[axis_at] // blocks).reshape((-1,) + (1,) * (len(extent) - axis_at - 1))

    loudness = one(*pieces[0])
    for cut in pieces[1:]:
        loudness = loudness * one(*cut)
    return loudness


def assign_block(own_key, own, number, rows, amount, top, bound, slope):
    sequence = jax.random.permutation(own_key, amount)
    packed, usual = portions_of(amount, rows * top, bound, slope, True), portions_of(amount, rows * top, bound, slope, False)
    places = jnp.arange(amount)

    def named(sizes, offset_by):
        used = int((sizes > 0).sum())
        fixed = max(1, used // 4)
        passed = fixed + (places - fixed + offset_by * (used - fixed)) % max(1, amount - fixed)
        return jnp.zeros((amount,), jnp.int32).at[sequence[jnp.where(places < fixed, places, passed)]].set(jnp.asarray(sizes, jnp.int32))

    sizes = jnp.where(number % 4 == 0, named(packed, number // 4), named(usual, number - number // 4 - 1))
    mixed = jax.random.permutation(jax.random.fold_in(own, 3), amount)
    donor, taker = mixed[0:amount // 2 * 2:2], mixed[1:amount // 2 * 2:2]
    margin = jnp.minimum(sizes[donor] - 1, bound - sizes[taker]) // 2
    margin = jnp.where((donor == sequence[0]) | (taker == sequence[0]) | (sizes[taker] == 0), 0, jnp.maximum(margin, 0))
    passed = jax.random.randint(jax.random.fold_in(own, 4), (amount // 2,), 0, 1 << 20) % (margin + 1)
    sizes = sizes.at[donor].add(-passed).at[taker].add(passed)
    labels = jnp.searchsorted(jnp.cumsum(sizes), jnp.arange(rows * top), side="right").astype(jnp.int32)
    listing = labels.reshape(top, rows).T
    listing = listing[jax.random.permutation(jax.random.fold_in(own, 1), rows)]
    offset_by = jax.random.randint(jax.random.fold_in(own, 2), (rows, 1), 0, top)
    return jnp.take_along_axis(listing, (jnp.arange(top)[None, :] + offset_by) % top, axis=1)


def portions_of(count, total, most, slope, full):
    loads = [(1 << 20) // math.isqrt(rank ** slope) + 1 for rank in range(1, count + 1)]
    largest = most if full else min(most, max(-(-total // count), total * loads[0] // sum(loads)))
    least = 1 if total - largest >= count - 1 else 0
    given, rest = [largest] + [least] * (count - 1), total - largest - least * (count - 1)
    while rest > 0:
        free = [i for i in range(1, count) if given[i] < largest] or [i for i in range(1, count) if given[i] < most]
        mass, budget = sum([loads[i] for i in free]), rest
        for i in free:
            extra = min(most - given[i], max(1, budget * loads[i] // mass), rest)
            given[i] = given[i] + extra
            rest = rest - extra
    return np.array(given)


def scatter_about(stream_key, extent, spread, most, shards=(), kind=jnp.bfloat16):
    array = jax.random.normal(stream_key, extent, jnp.float32) * spread
    if len(shards) > 0:
        array = block_levels(stream_key, extent, shards, -0.22, 0.18) * array
    return jnp.clip(array, min=-most, max=most).astype(kind)


def setup_inputs(seed: int = 0, part: int = 0) -> dict:
    key_of = jax.random.split(jax.random.key(seed), 14)
    part_keys = jax.random.split(jax.random.fold_in(key_of[13], part), 14)
    queries = draw_queries(jax.random.fold_in(jax.random.fold_in(key_of[13], part), 71), part)
    latent_cache = draw_latent_cache(jax.random.fold_in(jax.random.fold_in(key_of[13], part), 71), part)
    new_latent = scatter_about(part_keys[2], (TOKENS, KD), 1.0, 6.0, ((0, 32),))
    lengths = place_ends(jax.random.randint(part_keys[3], (REQS,), 2, CTX + 1), jax.random.fold_in(part_keys[3], 1), 2, CTX).astype(jnp.int32)
    residual = scatter_about(part_keys[4], (TOKENS, D), 1.0, 6.0, ((0, 32),))
    norm_gain = jnp.clip(1.0 + 0.1 * jax.random.normal(key_of[5], (D,), jnp.float32), 0.5, 1.5)
    value_up = scatter_about(key_of[6], (H, LAT, VH), LAT ** -0.5, 0.25, ((0, 32),))
    output_proj = scatter_about(key_of[7], (H, VH, D), (H * VH // 16) ** -0.5, 0.1875, ((0, 32),))
    expert_ids_keys = jax.random.split(jax.random.fold_in(part_keys[8], 1), TOKENS // TOK_PD)
    expert_ids_turns = jax.random.permutation(jax.random.fold_in(part_keys[8], 3), TOKENS // TOK_PD)
    expert_ids = jax.vmap(lambda own, number: assign_block(jax.random.fold_in(part_keys[8], 2), own, number, TOK_PD, EXPERTS, TOP, CAP, 2))(expert_ids_keys, expert_ids_turns).reshape((TOKENS, TOP))
    expert_weights = jnp.clip(jnp.exp(math.log(0.4) - 2.0794415 * jax.random.uniform(part_keys[9], (TOKENS, TOP), jnp.float32) ** block_levels(part_keys[9], (TOKENS, TOP), ((0, 32),), -0.2, 0.2)), 0.05, 0.4)
    gate_proj = scatter_about(key_of[10], (EXPERTS, D, FF), D ** -0.5, 0.09375, ((0, 16), (2, 2)))
    up_proj = scatter_about(key_of[11], (EXPERTS, D, FF), D ** -0.5, 0.09375, ((0, 16), (2, 2)))
    down_proj = scatter_about(key_of[12], (EXPERTS, FF, D), FF ** -0.5, 0.1875, ((0, 16), (1, 2)))
    return dict(queries=queries, latent_cache=latent_cache, new_latent=new_latent, lengths=lengths, residual=residual, norm_gain=norm_gain, value_up=value_up, output_proj=output_proj, expert_ids=expert_ids, expert_weights=expert_weights, gate_proj=gate_proj, up_proj=up_proj, down_proj=down_proj)


norm_epsilon = 1e-06
masked_score = -1e+30

def latent_attention(query_steps, latent_cache, new_steps, lengths):
    highest = lax.Precision.HIGHEST
    factor = 1.0 / QKD ** 0.5
    query_wide = query_steps.astype(jnp.float32)
    cache_wide = latent_cache.astype(jnp.float32)
    fresh_wide = new_steps.astype(jnp.float32)
    cache_scores = jnp.einsum('rshk,rpk->rshp', query_wide, cache_wide, precision=highest) * factor
    fresh_scores = jnp.einsum('rshk,rqk->rshq', query_wide, fresh_wide, precision=highest) * factor
    cache_live = lax.broadcasted_iota(jnp.int32, cache_scores.shape, 3) < lengths.astype(jnp.int32)[:, None, None, None]
    fresh_live = lax.broadcasted_iota(jnp.int32, fresh_scores.shape, 3) <= lax.broadcasted_iota(jnp.int32, fresh_scores.shape, 1)
    cache_scores = jnp.where(cache_live, cache_scores, masked_score)
    fresh_scores = jnp.where(fresh_live, fresh_scores, masked_score)
    highest_score = jnp.maximum(lax.optimization_barrier(jnp.max(cache_scores, axis=3)), lax.optimization_barrier(jnp.max(fresh_scores, axis=3)))[..., None]
    cache_weight = jnp.where(cache_live, jnp.exp(cache_scores - highest_score), 0.0)
    fresh_weight = jnp.where(fresh_live, jnp.exp(fresh_scores - highest_score), 0.0)
    weight_sum = lax.optimization_barrier(jnp.sum(cache_weight, axis=3)) + lax.optimization_barrier(jnp.sum(fresh_weight, axis=3))
    cache_round = lax.optimization_barrier(cache_weight.astype(jnp.bfloat16)).astype(jnp.float32)
    fresh_round = lax.optimization_barrier(fresh_weight.astype(jnp.bfloat16)).astype(jnp.float32)
    merged = jnp.einsum('rshp,rpl->rshl', cache_round, cache_wide[:, :, :LAT], precision=highest)
    merged = merged + jnp.einsum('rshq,rql->rshl', fresh_round, fresh_wide[:, :, :LAT], precision=highest)
    return (merged / weight_sum[..., None]).astype(jnp.bfloat16)

def reference(queries, latent_cache, new_latent, lengths, residual, norm_gain, value_up, output_proj, expert_ids, expert_weights, gate_proj, up_proj, down_proj):
    highest = lax.Precision.HIGHEST
    query_steps = queries.reshape(REQS, STEPS, H, KD)
    new_steps = new_latent.reshape(REQS, STEPS, KD)
    latent_out = latent_attention(query_steps, latent_cache, new_steps, lengths).reshape(TOKENS, H, LAT)
    head_out = jnp.einsum('thl,hlv->thv', latent_out.astype(jnp.float32), value_up.astype(jnp.float32), precision=highest).astype(jnp.bfloat16)
    attention = jnp.dot(head_out.reshape(TOKENS, H * VH), output_proj.reshape(H * VH, D), preferred_element_type=jnp.float32)
    stream = residual.astype(jnp.float32) + attention
    mean_square = lax.optimization_barrier(jnp.mean(stream * stream, axis=1, keepdims=True))
    normed = (stream * lax.rsqrt(mean_square + norm_epsilon) * norm_gain[None, :]).astype(jnp.bfloat16)
    half_width = FF // N_SIDE
    expert_range = jnp.arange(EXPERTS, dtype=jnp.int32)

    def one_expert(carry, inputs):
        gate_weight, up_weight, down_weight, expert_index = inputs
        share = lax.optimization_barrier(jnp.sum(jnp.where(expert_ids == expert_index, expert_weights, 0.0), axis=1))
        result = jnp.zeros((TOKENS, D), jnp.float32)
        for half in range(N_SIDE):
            lower = half * half_width
            upper = lower + half_width
            gate_part = jnp.dot(normed, gate_weight[:, lower:upper], preferred_element_type=jnp.float32)
            up_part = jnp.dot(normed, up_weight[:, lower:upper], preferred_element_type=jnp.float32)
            hidden = (jax.nn.silu(gate_part) * up_part).astype(jnp.bfloat16)
            partial_value = jnp.dot(hidden, down_weight[lower:upper, :], preferred_element_type=jnp.float32).astype(jnp.bfloat16)
            result = result + lax.optimization_barrier(partial_value).astype(jnp.float32)
        return (carry + share[:, None] * result, None)
    mixture, unused = lax.scan(one_expert, jnp.zeros((TOKENS, D), jnp.float32), (gate_proj, up_proj, down_proj, expert_range))
    return (stream + mixture).astype(jnp.bfloat16)
```

```python
import functools

import jax
import jax.numpy as jnp
import numpy as np
from jax import lax
from jax.experimental import pallas as pl
from jax.experimental.pallas import tpu as pltpu
from jax.sharding import PartitionSpec as P

LAT = 512
QKD = 192
MESH = pl.DeviceIdType.MESH
NORM_EPSILON = 1e-06
MASKED = -1e30
BF = jnp.bfloat16
F32 = jnp.float32


def remote(src, dst, send, recv, ep, side):
    return pltpu.make_async_remote_copy(
        src_ref=src,
        dst_ref=dst,
        send_sem=send,
        recv_sem=recv,
        device_id={"ep": ep, "side": side},
        device_id_type=MESH,
    )


def column_tile(width):
    return max(t for t in (512, 256, 128) if width % t == 0)


def kernel(
    dims,
    q_ref, cache_ref, fresh_ref, live_ref, fresh_live_ref, resid_ref, gain_ref, share_ref, pick_ref, head_ref,
    uv_hbm, op_hbm, gate_hbm, up_hbm, down_hbm,
    out_ref,
    uv, op, gate, up, down, weight_sem,
    lat_send, lat_recv, lat_ss, lat_rs,
    sh_recv, sh_ss, sh_rs, sh_rows,
    flat, hidden, acc, slab, blocks, stream, normed,
    s_send, s_recv, s_ss, s_rs,
    p_send, p_recv, p_ss, p_rs,
    z_send, z_recv, z_ss, z_rs,
    c1, c1_ss, c1_rs, xbuf, c2_ss, c2_rs, c3_ss, c3_rs,
):
    ep_n, sides, plane, zn, tok, hpd = dims
    n = ep_n * sides
    ep = lax.axis_index("ep")
    side = lax.axis_index("side")
    me = ep * sides + side
    z, c = ep // plane, ep % plane
    other = 1 - side
    my_slot = (side * plane + c) * zn + z
    feature = op_hbm.shape[2]
    quarters, piece = blocks.shape[1] // tok, blocks.shape[2]
    tile = column_tile(feature)

    barrier = pltpu.get_barrier_semaphore()

    @pl.loop(1, n)
    def _(k):
        d = (me + k) % n
        pl.semaphore_signal(
            barrier, inc=1, device_id={"ep": d // sides, "side": d % sides}, device_id_type=MESH
        )

    loads = [
        pltpu.make_async_copy(uv_hbm, uv, weight_sem.at[0]),
        pltpu.make_async_copy(op_hbm.at[0], op, weight_sem.at[1]),
        pltpu.make_async_copy(gate_hbm.at[0], gate, weight_sem.at[2]),
        pltpu.make_async_copy(up_hbm.at[0], up, weight_sem.at[3]),
        pltpu.make_async_copy(down_hbm.at[0], down, weight_sem.at[4]),
    ]
    for load in loads:
        load.start()

    factor = 1.0 / QKD**0.5
    merged_all = []
    for r in range(q_ref.shape[0]):
        q, keys, fresh = q_ref[r], cache_ref[r], fresh_ref[r]
        dims_t = (((1,), (1,)), ((), ()))
        s1 = lax.dot_general(q, keys, dims_t, preferred_element_type=F32) * factor
        s2 = lax.dot_general(q, fresh, dims_t, preferred_element_type=F32) * factor
        live1 = live_ref[r] > 0.0
        live2 = fresh_live_ref[...] > 0.0
        s1 = jnp.where(live1, s1, MASKED)
        s2 = jnp.where(live2, s2, MASKED)
        top = jnp.maximum(
            jnp.max(s1, axis=1, keepdims=True), jnp.max(s2, axis=1, keepdims=True)
        )
        w1 = jnp.where(live1, jnp.exp(s1 - top), 0.0)
        w2 = jnp.where(live2, jnp.exp(s2 - top), 0.0)
        total = jnp.sum(w1, axis=1, keepdims=True) + jnp.sum(w2, axis=1, keepdims=True)
        merged = jnp.dot(w1.astype(BF), keys[:, :LAT], preferred_element_type=F32)
        merged = merged + jnp.dot(w2.astype(BF), fresh[:, :LAT], preferred_element_type=F32)
        merged = merged / total
        merged_all.append(merged.reshape(n, merged.shape[0] // n, LAT))
    lat_send[...] = jnp.concatenate(merged_all, axis=1).astype(BF)

    pl.semaphore_wait(barrier, n - 1)

    def lat_copy(d, slot):
        return remote(
            lat_send.at[d], lat_recv.at[slot], lat_ss.at[d], lat_rs.at[slot], d // sides, d % sides
        )

    def share_copy(d, slot):
        return remote(
            share_ref, sh_recv.at[slot], sh_ss.at[d], sh_rs.at[slot], d // sides, d % sides
        )

    @pl.loop(1, n)
    def _(k):
        d = (me + k) % n
        lat_copy(d, me).start()

    @pl.loop(1, n)
    def _(k):
        d = (me + k) % n
        share_copy(d, my_slot).start()

    lat_recv[me] = lat_send[me]
    sh_recv[my_slot] = share_ref[...]
    loads[0].wait()
    loads[1].wait()

    @pl.loop(1, n)
    def _(k):
        d = (me + k) % n
        lat_copy(d, d).wait_recv()

    arrived = lat_recv[...].reshape(lat_recv.shape[0] * lat_recv.shape[1], LAT)
    width = uv.shape[2]
    for h in range(hpd):
        raised = jnp.dot(arrived, uv[h], preferred_element_type=F32).astype(BF)
        for half in range(2):
            picked = jnp.dot(pick_ref[half] * head_ref[h], raised, preferred_element_type=F32)
            flat[half, :, h * width : (h + 1) * width] = picked.astype(BF)

    def scatter_sum(g, value):
        @pl.loop(0, feature // tile)
        def _(j):
            cols = pl.ds(pl.multiple_of(j * tile, tile), tile)
            part = value(other, cols)
            s_send[g, :, :, cols] = part.reshape(plane, zn * tok, tile).astype(BF)

        pair = remote(s_send.at[g], s_recv.at[g], s_ss.at[g], s_rs.at[g], ep, other)
        pair.start()

        @pl.loop(0, feature // tile)
        def _(j):
            cols = pl.ds(pl.multiple_of(j * tile, tile), tile)
            acc[:, :, cols] = value(side, cols).reshape(plane, zn * tok, tile)

        pair.wait_recv()

        def plane_copy(k, slot):
            peer = (c + k) % plane
            return remote(
                p_send.at[g, peer], p_recv.at[g, slot], p_ss.at[g, peer], p_rs.at[g, slot],
                z * plane + peer, side,
            )

        @pl.loop(1, plane)
        def _(k):
            peer = (c + k) % plane
            p_send[g, peer] = (acc[peer] + s_recv[g, peer].astype(F32)).astype(BF)
            plane_copy(k, c).start()

        slab[...] = acc[c] + s_recv[g, c].astype(F32)

        @pl.loop(1, plane)
        def _(k):
            peer = (c + k) % plane
            plane_copy(k, peer).wait_recv()
            slab[...] += p_recv[g, peer].astype(F32)

        for layer in range(zn):
            for a in range(quarters):
                blocks[layer, a * tok : (a + 1) * tok, :] = slab[
                    layer * tok : (layer + 1) * tok, a * piece : (a + 1) * piece
                ]
        z_send[g] = blocks[...].astype(BF)

        def z_copy(k, slot):
            peer = (z + k) % zn
            return remote(
                z_send.at[g, peer], z_recv.at[g, slot], z_ss.at[g, peer], z_rs.at[g, slot],
                peer * plane + c, side,
            )

        for k in range(1, zn):
            z_copy(k, z).start()
        result = blocks[z]
        for k in range(1, zn):
            peer = (z + k) % zn
            z_copy(k, peer).wait_recv()
            result = result + z_recv[g, peer].astype(F32)

        def finish():
            pair.wait_send()

            @pl.loop(1, plane)
            def _(k):
                plane_copy(k, c).wait_send()

            for k in range(1, zn):
                z_copy(k, z).wait_send()

        return result, finish

    def attention_part(half, cols):
        return jnp.dot(flat[half], op[:, cols], preferred_element_type=F32)

    attention, finish_attention = scatter_sum(0, attention_part)
    stream[...] = resid_ref[...] + attention

    square = jnp.zeros((tok, 1), F32)
    for a in range(quarters):
        rows = stream[a * tok : (a + 1) * tok, :]
        square = square + jnp.sum(rows * rows, axis=1, keepdims=True)
    scale = lax.rsqrt(square * (1.0 / feature) + NORM_EPSILON)
    for a in range(quarters):
        normed[a * tok : (a + 1) * tok, :] = (
            stream[a * tok : (a + 1) * tok, :] * scale * gain_ref[a * tok : (a + 1) * tok, :]
        )
    c1[z] = normed[...].astype(BF)

    def line_copy(k, slot):
        peer = (z + k) % zn
        return remote(
            c1.at[z], c1.at[slot], c1_ss.at[peer], c1_rs.at[slot], peer * plane + c, side
        )

    for k in range(1, zn):
        line_copy(k, z).start()

    @pl.loop(1, n)
    def _(k):
        d = (me + k) % n
        e, s = d // sides, d % sides
        share_copy(d, (s * plane + e % plane) * zn + e // plane).wait_recv()

    for slot in range(n):
        sh_rows[slot * tok : (slot + 1) * tok, :] = sh_recv[slot, :tok, :]
    lanes = lax.broadcasted_iota(jnp.int32, sh_rows.shape, 1)
    share = jnp.sum(jnp.where(lanes == ep, sh_rows[...], 0.0), axis=1, keepdims=True)
    sh_rows[...] = jnp.broadcast_to(share, sh_rows.shape)

    for k in range(1, zn):
        peer = (z + k) % zn
        line_copy(k, peer).wait_recv()
    for layer in range(zn):
        blocks[layer] = c1[layer].astype(F32)
    for layer in range(zn):
        for a in range(quarters):
            slab[layer * tok : (layer + 1) * tok, a * piece : (a + 1) * piece] = blocks[
                layer, a * tok : (a + 1) * tok, :
            ]
    xbuf[side, c] = slab[...].astype(BF)

    def spread_copy(k, slot):
        peer = (c + k) % plane
        return remote(
            xbuf.at[side, c], xbuf.at[side, slot], c2_ss.at[peer], c2_rs.at[slot],
            z * plane + peer, side,
        )

    def pair_copy(slot, half):
        return remote(
            xbuf.at[half, slot], xbuf.at[half, slot], c3_ss.at[slot], c3_rs.at[slot], ep, other
        )

    @pl.loop(1, plane)
    def _(k):
        spread_copy(k, c).start()

    pair_copy(c, side).start()

    @pl.loop(1, plane)
    def _(k):
        peer = (c + k) % plane
        spread_copy(k, peer).wait_recv()
        pair_copy(peer, side).start()

    loads[2].wait()
    loads[3].wait()
    loads[4].wait()
    half_rows = plane * zn * tok

    def hidden_half(half):
        rows = xbuf[half].reshape(half_rows, feature)
        units = gate.shape[1]
        step = min(units, 256)
        for j in range(units // step):
            cols = slice(j * step, (j + 1) * step)
            gated = jnp.dot(rows, gate[:, cols], preferred_element_type=F32)
            raised = jnp.dot(rows, up[:, cols], preferred_element_type=F32)
            hidden[half, :, cols] = (gated / (1.0 + jnp.exp(-gated)) * raised).astype(BF)

    hidden_half(side)

    @pl.loop(0, plane)
    def _(k):
        pair_copy(k, other).wait_recv()

    hidden_half(other)

    def expert_part(half, cols):
        part = jnp.dot(hidden[half], down[:, cols], preferred_element_type=F32)
        rows = pl.ds(pl.multiple_of(half * half_rows, half_rows), half_rows)
        return part.astype(BF).astype(F32) * sh_rows[rows, :1]

    mixture, finish_mixture = scatter_sum(1, expert_part)
    out_ref[...] = (stream[...] + mixture).astype(BF)

    finish_attention()
    finish_mixture()

    @pl.loop(1, n)
    def _(k):
        d = (me + k) % n
        lat_copy(d, me).wait_send()
        share_copy(d, my_slot).wait_send()

    for k in range(1, zn):
        line_copy(k, z).wait_send()

    @pl.loop(1, plane)
    def _(k):
        spread_copy(k, c).wait_send()

    @pl.loop(0, plane)
    def _(k):
        pair_copy(k, side).wait_send()


def local(
    queries, latent_cache, new_latent, lengths, residual, norm_gain, value_up, output_proj,
    expert_ids, expert_weights, gate_proj, up_proj, down_proj,
):
    ep_n, sides = lax.axis_size("ep"), lax.axis_size("side")
    n = ep_n * sides
    requests, context, key_width = latent_cache.shape
    tok, head_count, _ = queries.shape
    steps = tok // requests
    hpd = value_up.shape[0]
    feature = residual.shape[1]
    plane = 1
    while plane * plane < ep_n:
        plane *= 2
    zn = ep_n // plane
    quarters = 16 // tok
    piece = feature // quarters
    rq = -(-steps * hpd // 8) * 8
    fresh_rows = 16

    q = queries.reshape(requests, steps, n, hpd, key_width).transpose(0, 2, 1, 3, 4)
    q = q.reshape(requests, n, steps * hpd, key_width)
    q = jnp.pad(q, ((0, 0), (0, 0), (0, rq - steps * hpd), (0, 0)))
    q = q.reshape(requests, n * rq, key_width)
    fresh = new_latent.reshape(requests, steps, key_width)
    fresh = jnp.pad(fresh, ((0, 0), (0, fresh_rows - steps), (0, 0)))
    live = (
        lax.broadcasted_iota(jnp.int32, (requests, 1, context), 2) < lengths[:, None, None]
    ).astype(F32)
    own_step = np.minimum((np.arange(n * rq) % rq) // hpd, steps - 1)
    fresh_live = (np.arange(fresh_rows)[None, :] <= own_step[:, None]).astype(np.float32)

    lat_rows = requests * rq
    pick = np.zeros((n, tok, n, lat_rows), np.float32)
    heads = np.zeros((hpd, n, lat_rows), np.float32)
    for d in range(n):
        e, s = d // sides, d % sides
        slot = (s * plane + e % plane) * zn + e // plane
        for t in range(tok):
            first = (t // steps) * rq + (t % steps) * hpd
            pick[slot, t, d, first : first + hpd] = 1.0
    for r in range(requests):
        for j in range(steps):
            for h in range(hpd):
                heads[h, :, r * rq + j * hpd + h] = 1.0
    pick = jnp.asarray(pick.reshape(sides, n * tok // sides, n * lat_rows), BF)
    heads = jnp.asarray(heads.reshape(hpd, 1, n * lat_rows), BF)

    def blocked(rows):
        return rows.reshape(tok, quarters, piece).transpose(1, 0, 2).reshape(quarters * tok, piece)

    resid = blocked(residual.astype(F32))
    gain = blocked(jnp.broadcast_to(norm_gain[None, :], (tok, feature)))
    lanes = -(-ep_n // 128) * 128
    chosen = expert_ids[:, :, None] == lax.broadcasted_iota(jnp.int32, (1, 1, lanes), 2)
    share = jnp.sum(jnp.where(chosen, expert_weights[:, :, None], 0.0), axis=1)
    share = jnp.pad(share, ((0, 8 - tok), (0, 0)))

    op = output_proj.reshape(1, hpd * output_proj.shape[1], feature)
    values = value_up.shape[2]
    units = gate_proj.shape[2]
    half = n * tok // 2
    zr = zn * tok
    blk = quarters * tok
    dma, vm = pltpu.SemaphoreType.DMA, pltpu.VMEM
    scratch = [
        vm(value_up.shape, BF), vm((hpd * values, feature), BF),
        vm((feature, units), BF), vm((feature, units), BF), vm((units, feature), BF), dma((5,)),
        vm((n, lat_rows, LAT), BF), vm((n, lat_rows, LAT), BF), dma((n,)), dma((n,)),
        vm((n, 8, lanes), F32), dma((n,)), dma((n,)), vm((n * tok, lanes), F32),
        vm((2, half, hpd * values), BF), vm((2, half, units), BF), vm((plane, zr, feature), F32),
        vm((zr, feature), F32), vm((zn, blk, piece), F32), vm((blk, piece), F32), vm((blk, piece), F32),
        vm((2, plane, zr, feature), BF), vm((2, plane, zr, feature), BF), dma((2,)), dma((2,)),
        vm((2, plane, zr, feature), BF), vm((2, plane, zr, feature), BF), dma((2, plane)), dma((2, plane)),
        vm((2, zn, blk, piece), BF), vm((2, zn, blk, piece), BF), dma((2, zn)), dma((2, zn)),
        vm((zn, blk, piece), BF), dma((zn,)), dma((zn,)),
        vm((2, plane, zr, feature), BF), dma((plane,)), dma((plane,)), dma((plane,)), dma((plane,)),
    ]
    in_vmem = pl.BlockSpec(memory_space=pltpu.VMEM)
    in_hbm = pl.BlockSpec(memory_space=pl.ANY)

    body = functools.partial(kernel, (ep_n, sides, plane, zn, tok, hpd))
    out = pl.pallas_call(
        body,
        out_shape=jax.ShapeDtypeStruct((blk, piece), BF),
        in_specs=[in_vmem] * 10 + [in_hbm] * 5,
        out_specs=in_vmem,
        scratch_shapes=scratch,
        compiler_params=pltpu.CompilerParams(
            collective_id=0, has_side_effects=True, vmem_limit_bytes=60 * 2**20
        ),
    )(
        q, latent_cache, fresh, live, jnp.asarray(fresh_live), resid, gain, share, pick, heads,
        value_up, op, gate_proj, up_proj, down_proj,
    )
    return out.reshape(quarters, tok, piece).transpose(1, 0, 2).reshape(tok, feature)


def solution(mesh):
    rows = ("groups", "ep", "side")
    in_specs = (
        P(rows, None, None),
        P(rows, None, None),
        P(rows, None),
        P(rows),
        P(rows, None),
        P(),
        P(("ep", "side"), None, None),
        P(("ep", "side"), None, None),
        P(rows, None),
        P(rows, None),
        P("ep", None, "side"),
        P("ep", None, "side"),
        P("ep", "side", None),
    )
    return jax.shard_map(
        local, mesh=mesh, in_specs=in_specs, out_specs=P(rows, None), check_vma=False
    )
```

```python
import functools

import jax
import jax.numpy as jnp
import numpy as np
from jax import lax
from jax.experimental import pallas as pl
from jax.experimental.pallas import tpu as pltpu
from jax.sharding import PartitionSpec as P

LAT = 512
QKD = 192
MESH = pl.DeviceIdType.MESH
NORM_EPSILON = 1e-06
MASKED = -1e30
BF = jnp.bfloat16
F32 = jnp.float32


def remote(src, dst, send, recv, ep, side):
    return pltpu.make_async_remote_copy(
        src_ref=src,
        dst_ref=dst,
        send_sem=send,
        recv_sem=recv,
        device_id={"ep": ep, "side": side},
        device_id_type=MESH,
    )


def kernel(
    dims,
    q_ref, cache_ref, fresh_ref, lengths_ref, resid_ref, gain_ref, ids_ref, weights_ref,
    fresh_live_ref, perm_ref, pick_ref, head_ref, sel_ref,
    uv_hbm, op_hbm, gate_hbm, up_hbm, down_hbm,
    out_ref,
    uv, op, gate, up, down, weight_sem,
    fresh_rows, lat_send, lat_recv, lat_ss, lat_rs, raised,
    sh_send, sh_recv, sh_ss, sh_rs, sh_rows,
    flat, hidden, acc, slab, blocks, total, stream, gains, squares, rows_out,
    s_send, s_recv, s_ss, s_rs,
    p_send, p_recv, p_ss, p_rs,
    z_send, z_recv, z_ss, z_rs,
    xblk, xrows, l_ss, l_rs, c_ss, c_rs, x_ss, x_rs,
):
    ep_n, sides, plane, zn, tok, hpd = dims
    n = ep_n * sides
    ep = lax.axis_index("ep")
    side = lax.axis_index("side")
    me = ep * sides + side
    z, c = ep // plane, ep % plane
    other = 1 - side
    my_slot = (side * plane + c) * zn + z
    feature = op_hbm.shape[2]
    chunks, quarters, piece = total.shape[0], total.shape[1] // tok, total.shape[2]
    tile = quarters * piece
    values = uv_hbm.shape[2]

    barrier = pltpu.get_barrier_semaphore()

    @pl.loop(1, n)
    def _(k):
        d = (me + k) % n
        pl.semaphore_signal(
            barrier, inc=1, device_id={"ep": d // sides, "side": d % sides}, device_id_type=MESH
        )

    loads = [
        pltpu.make_async_copy(uv_hbm.at[h], uv.at[:, pl.ds(h * values, values)], weight_sem.at[h])
        for h in range(hpd)
    ] + [
        pltpu.make_async_copy(op_hbm.at[0], op, weight_sem.at[hpd]),
        pltpu.make_async_copy(gate_hbm.at[0], gate, weight_sem.at[hpd + 1]),
        pltpu.make_async_copy(up_hbm.at[0], up, weight_sem.at[hpd + 2]),
        pltpu.make_async_copy(down_hbm.at[0], down, weight_sem.at[hpd + 3]),
    ]
    for load in loads:
        load.start()

    factor = 1.0 / QKD**0.5
    requests = cache_ref.shape[0]
    steps = tok // requests
    fresh_rows[...] = jnp.zeros_like(fresh_rows)
    fresh_rows[:tok, :] = fresh_ref[...].astype(F32)
    fresh = fresh_rows[...].astype(BF)
    merged_all = []
    for r in range(requests):
        q = jnp.concatenate([q_ref[r * steps + j].T for j in range(steps)], axis=0)
        keys = cache_ref[r]
        dims_t = (((1,), (1,)), ((), ()))
        s1 = jnp.dot(q, keys, preferred_element_type=F32) * factor
        s2 = lax.dot_general(q, fresh, dims_t, preferred_element_type=F32) * factor
        live1 = lax.broadcasted_iota(jnp.int32, s1.shape, 1) < lengths_ref[r]
        live2 = fresh_live_ref[r] > 0.0
        s1 = jnp.where(live1, s1, MASKED)
        s2 = jnp.where(live2, s2, MASKED)
        top = jnp.maximum(
            jnp.max(s1, axis=1, keepdims=True), jnp.max(s2, axis=1, keepdims=True)
        )
        w1 = jnp.where(live1, jnp.exp(s1 - top), 0.0)
        w2 = jnp.where(live2, jnp.exp(s2 - top), 0.0)
        weight_sum = jnp.sum(w1, axis=1, keepdims=True) + jnp.sum(w2, axis=1, keepdims=True)
        merged = lax.dot_general(
            w1.astype(BF), keys[:LAT, :], dims_t, preferred_element_type=F32
        )
        merged = merged + jnp.dot(w2.astype(BF), fresh[:, :LAT], preferred_element_type=F32)
        merged = (merged / weight_sum).astype(BF)
        ordered = jnp.dot(perm_ref[...].astype(BF), merged, preferred_element_type=F32)
        merged_all.append(ordered.reshape(n, ordered.shape[0] // n, LAT))
    lat_send[...] = jnp.concatenate(merged_all, axis=1).astype(BF)

    pl.semaphore_wait(barrier, n - 1)

    def lat_copy(d, slot):
        return remote(
            lat_send.at[d], lat_recv.at[slot], lat_ss.at[d], lat_rs.at[slot], d // sides, d % sides
        )

    def share_copy(d, slot):
        return remote(
            sh_send, sh_recv.at[slot], sh_ss.at[d], sh_rs.at[slot], d // sides, d % sides
        )

    @pl.loop(1, n)
    def _(k):
        lat_copy((me + (k * 13) % n) % n, me).start()

    lanes = lax.broadcasted_iota(jnp.int32, (tok, sh_send.shape[1]), 1)
    shares = jnp.zeros((tok, sh_send.shape[1]), F32)
    for k in range(ids_ref.shape[1]):
        shares = shares + jnp.where(
            lanes == ids_ref[:, k : k + 1], weights_ref[:, k : k + 1], 0.0
        )
    sh_send[...] = jnp.zeros_like(sh_send)
    sh_send[:tok, :] = shares

    @pl.loop(1, n)
    def _(k):
        share_copy((me + k) % n, my_slot).start()

    lat_recv[me] = lat_send[me]
    sh_recv[my_slot] = sh_send[...]

    rows_out[...] = resid_ref[...].astype(F32)
    for j in range(chunks):
        for a in range(quarters):
            cols = slice(j * tile + a * piece, j * tile + (a + 1) * piece)
            stream[j, a * tok : (a + 1) * tok, :] = rows_out[:, cols]
            gains[j, a * tok : (a + 1) * tok, :] = jnp.broadcast_to(gain_ref[:, cols], (tok, piece))

    for load in loads[: hpd + 1]:
        load.wait()

    group = plane * sides
    lat_rows = lat_recv.shape[1]

    @pl.loop(0, zn)
    def _(k):
        layer = (z + k) % zn

        @pl.loop(0, group)
        def _(i):
            d = layer * group + i

            @pl.when(d != me)
            def _():
                lat_copy(d, d).wait_recv()

        arrived = lat_recv[pl.ds(layer * group, group)].reshape(group * lat_rows, LAT)
        up_rows = jnp.dot(arrived, uv[...], preferred_element_type=F32).astype(BF)
        raised[layer] = up_rows * head_ref[...].astype(BF)

    everyone = raised[...].reshape(zn * group * lat_rows, raised.shape[2])
    for half in range(2):
        flat[half] = jnp.dot(pick_ref[half].astype(BF), everyone, preferred_element_type=F32).astype(BF)

    def scatter_sum(g, value):
        def pair(j):
            return remote(s_send.at[g, j], s_recv.at[g, j], s_ss.at[g, j], s_rs.at[g, j], ep, other)

        def plane_copy(j, k, slot):
            peer = (c + k) % plane
            return remote(
                p_send.at[g, j, peer], p_recv.at[g, j, slot], p_ss.at[g, j, peer],
                p_rs.at[g, j, slot], z * plane + peer, side,
            )

        def z_copy(j, k, slot):
            peer = (z + k) % zn
            return remote(
                z_send.at[g, j, peer], z_recv.at[g, j, slot], z_ss.at[g, j, peer],
                z_rs.at[g, j, slot], peer * plane + c, side,
            )

        def produce(j):
            cols = pl.ds(pl.multiple_of(j * tile, tile), tile)
            s_send[g, j] = value(other, cols).reshape(plane, zn * tok, tile).astype(BF)
            pair(j).start()
            acc[j] = value(side, cols).reshape(plane, zn * tok, tile)

        def spread(j):
            pair(j).wait_recv()
            for k in range(1, plane):
                peer = (c + k) % plane
                p_send[g, j, peer] = (acc[j, peer] + s_recv[g, j, peer].astype(F32)).astype(BF)
                plane_copy(j, k, c).start()

        produce(0)

        @pl.loop(1, chunks)
        def _(j):
            produce(j)
            spread(j - 1)

        spread(chunks - 1)

        @pl.loop(0, chunks)
        def _(j):
            own = acc[j, c] + s_recv[g, j, c].astype(F32)
            for k in range(1, plane):
                peer = (c + k) % plane
                plane_copy(j, k, peer).wait_recv()
                own = own + p_recv[g, j, peer].astype(F32)
            slab[...] = own
            for layer in range(zn):
                for a in range(quarters):
                    blocks[layer, a * tok : (a + 1) * tok, :] = slab[
                        layer * tok : (layer + 1) * tok, a * piece : (a + 1) * piece
                    ]
            z_send[g, j] = blocks[...].astype(BF)
            total[j] = blocks[z]
            for k in range(1, zn):
                z_copy(j, k, z).start()

        @pl.loop(0, chunks)
        def _(j):
            result = total[j]
            for k in range(1, zn):
                peer = (z + k) % zn
                z_copy(j, k, peer).wait_recv()
                result = result + z_recv[g, j, peer].astype(F32)
            total[j] = result

        def finish():
            @pl.loop(0, chunks)
            def _(j):
                pair(j).wait_send()
                for k in range(1, plane):
                    plane_copy(j, k, c).wait_send()
                for k in range(1, zn):
                    z_copy(j, k, z).wait_send()

        return finish

    def attention_part(half, cols):
        return jnp.dot(flat[half], op[:, cols], preferred_element_type=F32)

    finish_attention = scatter_sum(0, attention_part)
    stream[...] = stream[...] + total[...]

    square = jnp.sum(jnp.sum(stream[...] * stream[...], axis=0), axis=1, keepdims=True)
    squares[...] = jnp.broadcast_to(square, squares.shape)
    token_square = squares[:tok, :]
    for a in range(1, quarters):
        token_square = token_square + squares[a * tok : (a + 1) * tok, :]
    scale = lax.rsqrt(token_square * (1.0 / feature) + NORM_EPSILON)
    for a in range(quarters):
        squares[a * tok : (a + 1) * tok, :] = scale
    for j in range(chunks):
        xblk[side, c, z, :, j * piece : (j + 1) * piece] = (
            stream[j] * squares[...] * gains[j]
        ).astype(BF)

    def line_copy(k, slot):
        peer = (z + k) % zn
        return remote(
            xblk.at[side, c, z], xblk.at[side, c, slot], l_ss.at[peer], l_rs.at[slot],
            peer * plane + c, side,
        )

    def plane_rows(k, slot, layer):
        peer = (c + k) % plane
        return remote(
            xblk.at[side, c, layer], xblk.at[side, slot, layer], c_ss.at[peer, layer],
            c_rs.at[slot, layer], z * plane + peer, side,
        )

    def pair_rows(slot, layer, half):
        return remote(
            xblk.at[half, slot, layer], xblk.at[half, slot, layer], x_ss.at[slot, layer],
            x_rs.at[slot, layer], ep, other,
        )

    def hand_on(layer):
        for k in range(1, plane):
            plane_rows(k, c, layer).start()
        pair_rows(c, layer, side).start()

    for k in range(1, zn):
        line_copy(k, z).start()
    hand_on(z)

    @pl.loop(1, n)
    def _(k):
        d = (me + k) % n
        e, s = d // sides, d % sides
        share_copy(d, (s * plane + e % plane) * zn + e // plane).wait_recv()

    for slot in range(n):
        sh_rows[slot * tok : (slot + 1) * tok, :] = sh_recv[slot, :tok, :]
    all_lanes = lax.broadcasted_iota(jnp.int32, sh_rows.shape, 1)
    share = jnp.sum(jnp.where(all_lanes == ep, sh_rows[...], 0.0), axis=1, keepdims=True)
    sh_rows[...] = jnp.broadcast_to(share, sh_rows.shape)

    @pl.loop(0, zn)
    def _(kz):
        layer = (z + kz) % zn

        @pl.when(kz + 1 < zn)
        def _():
            line_copy(kz + 1, (z + kz + 1) % zn).wait_recv()
            hand_on((z + kz + 1) % zn)

        for k in range(1, plane):
            peer = (c + k) % plane
            plane_rows(k, peer, layer).wait_recv()
            pair_rows(peer, layer, side).start()

    for load in loads[hpd + 1 :]:
        load.wait()
    half_rows = plane * zn * tok

    def hidden_half(half):
        travelled = xblk[half].reshape(half_rows * quarters, chunks * piece)
        for a in range(quarters):
            rows = jnp.dot(sel_ref[a].astype(BF), travelled, preferred_element_type=F32).astype(BF)
            for j in range(chunks):
                first = j * tile + a * piece
                xrows[:, first : first + piece] = rows[:, j * piece : (j + 1) * piece]
        units = gate.shape[1]
        step = min(units, 256)
        for j in range(units // step):
            cols = slice(j * step, (j + 1) * step)
            gated = jnp.dot(xrows[...], gate[:, cols], preferred_element_type=F32)
            lifted = jnp.dot(xrows[...], up[:, cols], preferred_element_type=F32)
            hidden[half, :, cols] = (gated / (1.0 + jnp.exp(-gated)) * lifted).astype(BF)

    hidden_half(side)

    @pl.loop(0, plane)
    def _(k):
        @pl.loop(0, zn)
        def _(layer):
            pair_rows(k, layer, other).wait_recv()

    hidden_half(other)

    def expert_part(half, cols):
        part = jnp.dot(hidden[half], down[:, cols], preferred_element_type=F32)
        rows = pl.ds(pl.multiple_of(half * half_rows, half_rows), half_rows)
        return part.astype(BF).astype(F32) * sh_rows[rows, :1]

    finish_mixture = scatter_sum(1, expert_part)
    stream[...] = stream[...] + total[...]
    for j in range(chunks):
        for a in range(quarters):
            cols = slice(j * tile + a * piece, j * tile + (a + 1) * piece)
            rows_out[:, cols] = stream[j, a * tok : (a + 1) * tok, :]
    out_ref[...] = rows_out[...].astype(BF)

    finish_attention()
    finish_mixture()

    @pl.loop(1, n)
    def _(k):
        d = (me + k) % n
        lat_copy(d, me).wait_send()
        share_copy(d, my_slot).wait_send()

    for k in range(1, zn):
        line_copy(k, z).wait_send()

    @pl.loop(0, zn)
    def _(layer):
        for k in range(1, plane):
            plane_rows(k, c, layer).wait_send()

        @pl.loop(0, plane)
        def _(slot):
            pair_rows(slot, layer, side).wait_send()


def local(
    queries, latent_cache, new_latent, lengths, residual, norm_gain, value_up, output_proj,
    expert_ids, expert_weights, gate_proj, up_proj, down_proj,
):
    ep_n, sides = lax.axis_size("ep"), lax.axis_size("side")
    n = ep_n * sides
    requests, context, key_width = latent_cache.shape
    tok, head_count, _ = queries.shape
    steps = tok // requests
    hpd = value_up.shape[0]
    feature = residual.shape[1]
    plane = 1
    while plane * plane < ep_n:
        plane *= 2
    zn = ep_n // plane
    quarters = 16 // tok
    piece = 128
    tile = quarters * piece
    chunks = feature // tile
    rq = -(-steps * hpd // 8) * 8
    fresh_count = 16
    lat_rows = requests * rq
    values = value_up.shape[2]
    units = gate_proj.shape[2]

    key = np.arange(fresh_count)[None, None, :]
    request = np.arange(requests)[:, None, None]
    step = (np.arange(steps * head_count) // head_count)[None, :, None]
    fresh_live = (key // steps == request) & (key % steps <= step) & (key < tok)

    perm = np.zeros((n, rq, steps * head_count), np.float32)
    for d in range(n):
        for j in range(steps):
            for h in range(hpd):
                perm[d, j * hpd + h, j * head_count + d * hpd + h] = 1.0
    perm = perm.reshape(n * rq, steps * head_count)

    pick = np.zeros((n, tok, n, lat_rows), np.float32)
    heads = np.zeros((plane * sides, lat_rows, hpd, values), np.float32)
    for d in range(n):
        e, s = d // sides, d % sides
        slot = (s * plane + e % plane) * zn + e // plane
        for t in range(tok):
            first = (t // steps) * rq + (t % steps) * hpd
            pick[slot, t, d, first : first + hpd] = 1.0
    for t in range(tok):
        for h in range(hpd):
            heads[:, (t // steps) * rq + (t % steps) * hpd + h, h] = 1.0
    pick = pick.reshape(sides, n * tok // sides, n * lat_rows)
    heads = heads.reshape(plane * sides * lat_rows, hpd * values)

    slots = ep_n
    sel = np.zeros((quarters, slots, tok, slots, quarters, tok), np.float32)
    for a in range(quarters):
        for slot in range(slots):
            for t in range(tok):
                sel[a, slot, t, slot, a, t] = 1.0
    sel = sel.reshape(quarters, slots * tok, slots * quarters * tok)

    lanes = -(-ep_n // 128) * 128
    op = output_proj.reshape(1, hpd * output_proj.shape[1], feature)
    half = n * tok // 2
    zr = zn * tok
    blk = quarters * tok
    dma, vm = pltpu.SemaphoreType.DMA, pltpu.VMEM
    scratch = [
        vm((LAT, hpd * values), BF), vm((hpd * values, feature), BF),
        vm((feature, units), BF), vm((feature, units), BF), vm((units, feature), BF), dma((hpd + 4,)),
        vm((fresh_count, key_width), F32),
        vm((n, lat_rows, LAT), BF), vm((n, lat_rows, LAT), BF), dma((n,)), dma((n,)),
        vm((zn, plane * sides * lat_rows, hpd * values), BF),
        vm((8, lanes), F32), vm((n, 8, lanes), F32), dma((n,)), dma((n,)), vm((n * tok, lanes), F32),
        vm((2, half, hpd * values), BF), vm((2, half, units), BF),
        vm((chunks, plane, zr, tile), F32), vm((zr, tile), F32), vm((zn, blk, piece), F32),
        vm((chunks, blk, piece), F32), vm((chunks, blk, piece), F32), vm((chunks, blk, piece), F32),
        vm((blk, piece), F32), vm((tok, feature), F32),
        vm((2, chunks, plane, zr, tile), BF), vm((2, chunks, plane, zr, tile), BF),
        dma((2, chunks)), dma((2, chunks)),
        vm((2, chunks, plane, zr, tile), BF), vm((2, chunks, plane, zr, tile), BF),
        dma((2, chunks, plane)), dma((2, chunks, plane)),
        vm((2, chunks, zn, blk, piece), BF), vm((2, chunks, zn, blk, piece), BF),
        dma((2, chunks, zn)), dma((2, chunks, zn)),
        vm((sides, plane, zn, blk, chunks * piece), BF), vm((half, feature), BF),
        dma((zn,)), dma((zn,)), dma((plane, zn)), dma((plane, zn)), dma((plane, zn)), dma((plane, zn)),
    ]
    in_vmem = pl.BlockSpec(memory_space=pltpu.VMEM)
    in_smem = pl.BlockSpec(memory_space=pltpu.SMEM)
    in_hbm = pl.BlockSpec(memory_space=pl.ANY)
    body = functools.partial(kernel, (ep_n, sides, plane, zn, tok, hpd))
    return pl.pallas_call(
        body,
        out_shape=jax.ShapeDtypeStruct((tok, feature), BF),
        in_specs=[in_vmem] * 3 + [in_smem] + [in_vmem] * 9 + [in_hbm] * 5,
        out_specs=in_vmem,
        scratch_shapes=scratch,
        compiler_params=pltpu.CompilerParams(
            collective_id=0, has_side_effects=True, vmem_limit_bytes=60 * 2**20
        ),
    )(
        queries.transpose(0, 2, 1), latent_cache.transpose(0, 2, 1), new_latent, lengths, residual,
        norm_gain.reshape(1, feature),
        expert_ids, expert_weights, jnp.asarray(fresh_live, F32), jnp.asarray(perm),
        jnp.asarray(pick), jnp.asarray(heads), jnp.asarray(sel),
        value_up, op, gate_proj, up_proj, down_proj,
    )


def solution(mesh):
    rows = ("groups", "ep", "side")
    in_specs = (
        P(rows, None, None),
        P(rows, None, None),
        P(rows, None),
        P(rows),
        P(rows, None),
        P(),
        P(("ep", "side"), None, None),
        P(("ep", "side"), None, None),
        P(rows, None),
        P(rows, None),
        P("ep", None, "side"),
        P("ep", None, "side"),
        P("ep", "side", None),
    )
    return jax.shard_map(
        local, mesh=mesh, in_specs=in_specs, out_specs=P(rows, None), check_vma=False
    )
```

```python
import functools

import jax
import jax.numpy as jnp
import numpy as np
from jax import lax
from jax.experimental import pallas as pl
from jax.experimental.pallas import tpu as pltpu
from jax.sharding import PartitionSpec as P

LAT = 512
QKD = 192
MESH = pl.DeviceIdType.MESH
NORM_EPSILON = 1e-06
MASKED = -1e30
BF = jnp.bfloat16
F32 = jnp.float32


def remote(src, dst, send, recv, ep, side):
    return pltpu.make_async_remote_copy(
        src_ref=src,
        dst_ref=dst,
        send_sem=send,
        recv_sem=recv,
        device_id={"ep": ep, "side": side},
        device_id_type=MESH,
    )


def kernel(
    dims,
    q_ref, cache_ref, fresh_ref, lengths_ref, resid_ref, gain_ref, ids_ref, weights_ref,
    fresh_live_ref, perm_ref, pick_ref, head_ref, sel_ref,
    uv_hbm, op_hbm, gate_hbm, up_hbm, down_hbm,
    out_ref,
    uv, op, gate, up, down, weight_sem,
    fresh_rows, lat_send, lat_recv, lat_ss, lat_rs, raised,
    shares, sh_rows,
    flat, hidden, acc, slab, blocks, total, stream, gains, squares, rows_out,
    s_send, s_recv, s_ss, s_rs,
    p_send, p_recv, p_ss, p_rs,
    z_send, z_recv, z_ss, z_rs,
    xblk, xrows, l_ss, l_rs, c_ss, c_rs, x_ss, x_rs,
):
    ep_n, sides, plane, zn, tok, hpd = dims
    n = ep_n * sides
    ep = lax.axis_index("ep")
    side = lax.axis_index("side")
    me = ep * sides + side
    z, c = ep // plane, ep % plane
    other = 1 - side
    feature = op_hbm.shape[2]
    chunks, quarters, piece = total.shape[0], total.shape[1] // tok, total.shape[2]
    tile = quarters * piece
    values = uv_hbm.shape[2]

    barrier = pltpu.get_barrier_semaphore()

    @pl.loop(1, n)
    def _(k):
        d = (me + k) % n
        pl.semaphore_signal(
            barrier, inc=1, device_id={"ep": d // sides, "side": d % sides}, device_id_type=MESH
        )

    loads = [
        pltpu.make_async_copy(uv_hbm.at[h], uv.at[:, pl.ds(h * values, values)], weight_sem.at[h])
        for h in range(hpd)
    ] + [
        pltpu.make_async_copy(op_hbm.at[0], op, weight_sem.at[hpd]),
        pltpu.make_async_copy(gate_hbm.at[0], gate, weight_sem.at[hpd + 1]),
        pltpu.make_async_copy(up_hbm.at[0], up, weight_sem.at[hpd + 2]),
        pltpu.make_async_copy(down_hbm.at[0], down, weight_sem.at[hpd + 3]),
    ]
    for load in loads:
        load.start()

    factor = 1.0 / QKD**0.5
    requests = cache_ref.shape[0]
    steps = tok // requests
    fresh_rows[...] = jnp.zeros_like(fresh_rows)
    fresh_rows[:tok, :] = fresh_ref[...].astype(F32)
    fresh = fresh_rows[...].astype(BF)
    merged_all = []
    for r in range(requests):
        q = jnp.concatenate([q_ref[r * steps + j].T for j in range(steps)], axis=0)
        keys = cache_ref[r]
        dims_t = (((1,), (1,)), ((), ()))
        s1 = jnp.dot(q, keys, preferred_element_type=F32) * factor
        s2 = lax.dot_general(q, fresh, dims_t, preferred_element_type=F32) * factor
        live1 = lax.broadcasted_iota(jnp.int32, s1.shape, 1) < lengths_ref[r]
        live2 = fresh_live_ref[r] > 0.0
        s1 = jnp.where(live1, s1, MASKED)
        s2 = jnp.where(live2, s2, MASKED)
        top = jnp.maximum(
            jnp.max(s1, axis=1, keepdims=True), jnp.max(s2, axis=1, keepdims=True)
        )
        w1 = jnp.where(live1, jnp.exp(s1 - top), 0.0)
        w2 = jnp.where(live2, jnp.exp(s2 - top), 0.0)
        weight_sum = jnp.sum(w1, axis=1, keepdims=True) + jnp.sum(w2, axis=1, keepdims=True)
        merged = lax.dot_general(
            w1.astype(BF), keys[:LAT, :], dims_t, preferred_element_type=F32
        )
        merged = merged + jnp.dot(w2.astype(BF), fresh[:, :LAT], preferred_element_type=F32)
        merged = (merged / weight_sum).astype(BF)
        ordered = jnp.dot(perm_ref[...].astype(BF), merged, preferred_element_type=F32)
        merged_all.append(ordered.reshape(n, ordered.shape[0] // n, LAT))
    lat_send[...] = jnp.concatenate(merged_all, axis=1).astype(BF)

    pl.semaphore_wait(barrier, n - 1)

    def lat_copy(d, slot):
        return remote(
            lat_send.at[d], lat_recv.at[slot], lat_ss, lat_rs.at[z], d // sides, d % sides
        )

    @pl.loop(1, n)
    def _(k):
        lat_copy((me + (k * 13) % n) % n, me).start()

    lat_recv[me] = lat_send[me]

    lanes = lax.broadcasted_iota(jnp.int32, (tok, shares.shape[1]), 1)
    share = jnp.zeros((tok, shares.shape[1]), F32)
    for k in range(ids_ref.shape[1]):
        share = share + jnp.where(lanes == ids_ref[:, k : k + 1], weights_ref[:, k : k + 1], 0.0)
    shares[...] = jnp.zeros_like(shares)
    for a in range(3):
        term = share.astype(BF).astype(F32)
        shares[a * tok : (a + 1) * tok, :] = term
        share = share - term
    xblk[side, z, c, :, chunks * piece :] = shares[...].astype(BF)

    rows_out[...] = resid_ref[...].astype(F32)
    for j in range(chunks):
        for a in range(quarters):
            cols = slice(j * tile + a * piece, j * tile + (a + 1) * piece)
            stream[j, a * tok : (a + 1) * tok, :] = rows_out[:, cols]
            gains[j, a * tok : (a + 1) * tok, :] = jnp.broadcast_to(
                gain_ref[cols][None, :], (tok, piece)
            )

    for load in loads[: hpd + 1]:
        load.wait()

    group = plane * sides
    lat_rows = lat_recv.shape[1]

    for k in range(zn):
        layer = (z + k) % zn
        got = lat_recv.at[pl.ds(layer * group, group if k else group - 1)]
        remote(got, got, lat_ss, lat_rs.at[layer], ep, other).wait_recv()
        arrived = lat_recv[pl.ds(layer * group, group)].reshape(group * lat_rows, LAT)
        up_rows = jnp.dot(arrived, uv[...], preferred_element_type=F32).astype(BF)
        raised[layer] = up_rows * head_ref[...].astype(BF)

    everyone = raised[...].reshape(zn * group * lat_rows, raised.shape[2])
    flat[...] = jnp.dot(pick_ref[...].astype(BF), everyone, preferred_element_type=F32).astype(BF)

    cut = -(-chunks // 2)
    groups = ((0, cut), (cut, chunks - cut))

    def scatter_sum(g, value):
        def pair(i):
            part = pl.ds(*groups[i])
            return remote(
                s_send.at[g, part], s_recv.at[g, part], s_ss.at[g, i], s_rs.at[g, i], ep, other
            )

        def plane_copy(i, k):
            peer, part = (c + k) % plane, pl.ds(*groups[i])
            return remote(
                p_send.at[g, peer, part], p_recv.at[g, c, part], p_ss.at[g, i], p_rs.at[g, i],
                z * plane + peer, side,
            )

        def z_copy(i, k):
            peer, part = (z + k) % zn, pl.ds(*groups[i])
            return remote(
                z_send.at[g, peer, part], z_recv.at[g, z, part], z_ss.at[g, i], z_rs.at[g, i],
                peer * plane + c, side,
            )

        def all_plane(i):
            some, part = pl.ds(0, plane - 1), pl.ds(*groups[i])
            return remote(
                p_send.at[g, some, part], p_recv.at[g, some, part], p_ss.at[g, i], p_rs.at[g, i],
                ep, other,
            )

        def all_z(i):
            some, part = pl.ds(0, zn - 1), pl.ds(*groups[i])
            return remote(
                z_send.at[g, some, part], z_recv.at[g, some, part], z_ss.at[g, i], z_rs.at[g, i],
                ep, other,
            )

        def chunk_loop(i):
            return pl.loop(groups[i][0], groups[i][0] + groups[i][1])

        for i in range(2):

            @chunk_loop(i)
            def _(j):
                cols = pl.ds(pl.multiple_of(j * tile, tile), tile)
                acc[j] = value(cols).reshape(sides, plane, zn * tok, tile)
                s_send[g, j] = acc[j, other].astype(BF)

            pair(i).start()

        for i in range(2):
            pair(i).wait_recv()
            for k in range(1, plane):
                peer = (c + k) % plane

                @chunk_loop(i)
                def _(j):
                    p_send[g, peer, j] = (
                        acc[j, side, peer] + s_recv[g, j, peer].astype(F32)
                    ).astype(BF)

                plane_copy(i, k).start()

        for i in range(2):
            all_plane(i).wait_recv()

            @chunk_loop(i)
            def _(j):
                own = acc[j, side, c] + s_recv[g, j, c].astype(F32)
                for k in range(1, plane):
                    own = own + p_recv[g, (c + k) % plane, j].astype(F32)
                slab[...] = own
                for layer in range(zn):
                    for a in range(quarters):
                        blocks[layer, a * tok : (a + 1) * tok, :] = slab[
                            layer * tok : (layer + 1) * tok, a * piece : (a + 1) * piece
                        ]
                for layer in range(zn):
                    z_send[g, layer, j] = blocks[layer].astype(BF)
                total[j] = blocks[z]

            for k in range(1, zn):
                z_copy(i, k).start()

        for i in range(2):
            all_z(i).wait_recv()

            @chunk_loop(i)
            def _(j):
                result = total[j]
                for k in range(1, zn):
                    result = result + z_recv[g, (z + k) % zn, j].astype(F32)
                total[j] = result

        def finish():
            for i in range(2):
                pair(i).wait_send()
                all_plane(i).wait_send()
                all_z(i).wait_send()

        return finish

    def attention_part(cols):
        return jnp.dot(flat[...], op[:, cols], preferred_element_type=F32)

    finish_attention = scatter_sum(0, attention_part)
    stream[...] = stream[...] + total[...]

    square = jnp.sum(jnp.sum(stream[...] * stream[...], axis=0), axis=1, keepdims=True)
    squares[...] = jnp.broadcast_to(square, squares.shape)
    token_square = squares[:tok, :]
    for a in range(1, quarters):
        token_square = token_square + squares[a * tok : (a + 1) * tok, :]
    scale = lax.rsqrt(token_square * (1.0 / feature) + NORM_EPSILON)
    for a in range(quarters):
        squares[a * tok : (a + 1) * tok, :] = scale
    for j in range(chunks):
        xblk[side, z, c, :, j * piece : (j + 1) * piece] = (
            stream[j] * squares[...] * gains[j]
        ).astype(BF)

    def line_copy(k, slot):
        peer = (z + k) % zn
        return remote(
            xblk.at[side, z, c], xblk.at[side, slot, c], l_ss.at[peer], l_rs.at[slot],
            peer * plane + c, side,
        )

    def plane_rows(k, layer):
        return remote(
            xblk.at[side, layer, c], xblk.at[side, layer, c], c_ss.at[layer], c_rs.at[layer],
            z * plane + (c + k) % plane, side,
        )

    def plane_all(layer):
        some = xblk.at[side, layer, pl.ds(0, plane - 1)]
        return remote(some, some, c_ss.at[layer], c_rs.at[layer], ep, other)

    def pair_rows(layer, half):
        return remote(
            xblk.at[half, layer], xblk.at[half, layer], x_ss.at[layer], x_rs.at[layer], ep, other
        )

    for k in range(1, zn):
        line_copy(k, z).start()
    for k in range(1, plane):
        plane_rows(k, z).start()
    for kz in range(zn):
        layer, following = (z + kz) % zn, (z + kz + 1) % zn
        if kz + 1 < zn:
            line_copy(kz + 1, following).wait_recv()
            for k in range(1, plane):
                plane_rows(k, following).start()
        plane_all(layer).wait_recv()
        pair_rows(layer, side).start()

    for load in loads[hpd + 1 :]:
        load.wait()
    half_rows = plane * zn * tok

    def unpack(half):
        travelled = xblk[half].reshape(half_rows * quarters, xblk.shape[4])
        rows = jnp.dot(sel_ref[...].astype(BF), travelled, preferred_element_type=F32)
        for a in range(quarters):
            for j in range(chunks):
                first = j * tile + a * piece
                xrows[half, :, first : first + piece] = rows[
                    a * half_rows : (a + 1) * half_rows, j * piece : (j + 1) * piece
                ].astype(BF)
        terms = rows[:half_rows, chunks * piece :]
        for a in range(1, 3):
            terms = terms + rows[a * half_rows : (a + 1) * half_rows, chunks * piece :]
        which = lax.broadcasted_iota(jnp.int32, terms.shape, 1)
        weight = jnp.sum(jnp.where(which == ep, terms, 0.0), axis=1, keepdims=True)
        sh_rows[half] = jnp.broadcast_to(weight, sh_rows.shape[1:])

    unpack(side)
    for layer in range(zn):
        pair_rows(layer, other).wait_recv()
    unpack(other)

    units = gate.shape[1]
    step = min(units, 256)
    everything = xrows[...].reshape(sides * half_rows, feature)
    for j in range(units // step):
        cols = slice(j * step, (j + 1) * step)
        gated = jnp.dot(everything, gate[:, cols], preferred_element_type=F32)
        lifted = jnp.dot(everything, up[:, cols], preferred_element_type=F32)
        hidden[:, cols] = (gated / (1.0 + jnp.exp(-gated)) * lifted).astype(BF)

    def expert_part(cols):
        part = jnp.dot(hidden[...], down[:, cols], preferred_element_type=F32)
        weight = sh_rows[...].reshape(sides * half_rows, sh_rows.shape[2])[:, :1]
        return part.astype(BF).astype(F32) * weight

    finish_mixture = scatter_sum(1, expert_part)
    stream[...] = stream[...] + total[...]
    for j in range(chunks):
        for a in range(quarters):
            cols = slice(j * tile + a * piece, j * tile + (a + 1) * piece)
            rows_out[:, cols] = stream[j, a * tok : (a + 1) * tok, :]
    out_ref[...] = rows_out[...].astype(BF)

    finish_attention()
    finish_mixture()
    sent = lat_send.at[pl.ds(0, n - 1)]
    remote(sent, sent, lat_ss, lat_rs.at[0], ep, other).wait_send()
    for k in range(1, zn):
        line_copy(k, z).wait_send()
    for layer in range(zn):
        plane_all(layer).wait_send()
        pair_rows(layer, side).wait_send()


def local(
    queries, latent_cache, new_latent, lengths, residual, norm_gain, value_up, output_proj,
    expert_ids, expert_weights, gate_proj, up_proj, down_proj,
):
    ep_n, sides = lax.axis_size("ep"), lax.axis_size("side")
    n = ep_n * sides
    requests, context, key_width = latent_cache.shape
    tok, head_count, _ = queries.shape
    steps = tok // requests
    hpd = value_up.shape[0]
    feature = residual.shape[1]
    plane = 1
    while plane * plane < ep_n:
        plane *= 2
    zn = ep_n // plane
    quarters = 16 // tok
    piece = 128
    tile = quarters * piece
    chunks = feature // tile
    rq = -(-steps * hpd // 8) * 8
    fresh_count = 16
    lat_rows = requests * rq
    values = value_up.shape[2]
    units = gate_proj.shape[2]

    key = np.arange(fresh_count)[None, None, :]
    request = np.arange(requests)[:, None, None]
    step = (np.arange(steps * head_count) // head_count)[None, :, None]
    fresh_live = (key // steps == request) & (key % steps <= step) & (key < tok)

    perm = np.zeros((n, rq, steps * head_count), np.float32)
    for d in range(n):
        for j in range(steps):
            for h in range(hpd):
                perm[d, j * hpd + h, j * head_count + d * hpd + h] = 1.0
    perm = perm.reshape(n * rq, steps * head_count)

    pick = np.zeros((n, tok, n, lat_rows), np.float32)
    heads = np.zeros((plane * sides, lat_rows, hpd, values), np.float32)
    for d in range(n):
        e, s = d // sides, d % sides
        slot = (s * plane + e % plane) * zn + e // plane
        for t in range(tok):
            first = (t // steps) * rq + (t % steps) * hpd
            pick[slot, t, d, first : first + hpd] = 1.0
    for t in range(tok):
        for h in range(hpd):
            heads[:, (t // steps) * rq + (t % steps) * hpd + h, h] = 1.0
    pick = pick.reshape(n * tok, n * lat_rows)
    heads = heads.reshape(plane * sides * lat_rows, hpd * values)

    sel = np.zeros((quarters, plane, zn, tok, zn, plane, quarters, tok), np.float32)
    for a in range(quarters):
        for e in range(ep_n):
            for t in range(tok):
                sel[a, e % plane, e // plane, t, e // plane, e % plane, a, t] = 1.0
    sel = sel.reshape(quarters * ep_n * tok, ep_n * quarters * tok)

    lanes = -(-ep_n // 128) * 128
    op = output_proj.reshape(1, hpd * output_proj.shape[1], feature)
    half = n * tok // 2
    zr = zn * tok
    blk = quarters * tok
    dma, vm = pltpu.SemaphoreType.DMA, pltpu.VMEM
    scratch = [
        vm((LAT, hpd * values), BF), vm((hpd * values, feature), BF),
        vm((feature, units), BF), vm((feature, units), BF), vm((units, feature), BF), dma((hpd + 4,)),
        vm((fresh_count, key_width), F32),
        vm((n, lat_rows, LAT), BF), vm((n, lat_rows, LAT), BF), dma(()), dma((zn,)),
        vm((zn, plane * sides * lat_rows, hpd * values), BF),
        vm((blk, lanes), F32), vm((sides, half, lanes), F32),
        vm((2 * half, hpd * values), BF), vm((2 * half, units), BF),
        vm((chunks, sides, plane, zr, tile), F32), vm((zr, tile), F32), vm((zn, blk, piece), F32),
        vm((chunks, blk, piece), F32), vm((chunks, blk, piece), F32), vm((chunks, blk, piece), F32),
        vm((blk, piece), F32), vm((tok, feature), F32),
        vm((2, chunks, plane, zr, tile), BF), vm((2, chunks, plane, zr, tile), BF),
        dma((2, 2)), dma((2, 2)),
        vm((2, plane, chunks, zr, tile), BF), vm((2, plane, chunks, zr, tile), BF),
        dma((2, 2)), dma((2, 2)),
        vm((2, zn, chunks, blk, piece), BF), vm((2, zn, chunks, blk, piece), BF),
        dma((2, 2)), dma((2, 2)),
        vm((sides, zn, plane, blk, chunks * piece + lanes), BF), vm((sides, half, feature), BF),
        dma((zn,)), dma((zn,)), dma((zn,)), dma((zn,)), dma((zn,)), dma((zn,)),
    ]
    in_vmem = pl.BlockSpec(memory_space=pltpu.VMEM)
    in_smem = pl.BlockSpec(memory_space=pltpu.SMEM)
    in_hbm = pl.BlockSpec(memory_space=pl.ANY)
    body = functools.partial(kernel, (ep_n, sides, plane, zn, tok, hpd))
    return pl.pallas_call(
        body,
        out_shape=jax.ShapeDtypeStruct((tok, feature), BF),
        in_specs=[in_vmem] * 3 + [in_smem] + [in_vmem] * 9 + [in_hbm] * 5,
        out_specs=in_vmem,
        scratch_shapes=scratch,
        compiler_params=pltpu.CompilerParams(
            collective_id=0, has_side_effects=True, vmem_limit_bytes=60 * 2**20
        ),
    )(
        queries.transpose(0, 2, 1), latent_cache.transpose(0, 2, 1), new_latent, lengths, residual,
        norm_gain,
        expert_ids, expert_weights, jnp.asarray(fresh_live, F32), jnp.asarray(perm),
        jnp.asarray(pick), jnp.asarray(heads), jnp.asarray(sel),
        value_up, op, gate_proj, up_proj, down_proj,
    )


def solution(mesh):
    rows = ("groups", "ep", "side")
    in_specs = (
        P(rows, None, None),
        P(rows, None, None),
        P(rows, None),
        P(rows),
        P(rows, None),
        P(),
        P(("ep", "side"), None, None),
        P(("ep", "side"), None, None),
        P(rows, None),
        P(rows, None),
        P("ep", None, "side"),
        P("ep", None, "side"),
        P("ep", "side", None),
    )
    return jax.shard_map(
        local, mesh=mesh, in_specs=in_specs, out_specs=P(rows, None), check_vma=False
    )
```

```python
import functools

import jax
import jax.numpy as jnp
import numpy as np
from jax import lax
from jax.experimental import pallas as pl
from jax.experimental.pallas import tpu as pltpu
from jax.sharding import PartitionSpec as P

LAT = 512
QKD = 192
MESH = pl.DeviceIdType.MESH
NORM_EPSILON = 1e-06
MASKED = -1e30
BF = jnp.bfloat16
F32 = jnp.float32


def remote(src, dst, send, recv, ep, side):
    return pltpu.make_async_remote_copy(
        src_ref=src,
        dst_ref=dst,
        send_sem=send,
        recv_sem=recv,
        device_id={"ep": ep, "side": side},
        device_id_type=MESH,
    )


def kernel(
    dims,
    q_ref, cache_ref, fresh_ref, lengths_ref, resid_ref, gain_ref, ids_ref, weights_ref,
    fresh_live_ref, perm_ref, pick_ref, head_ref, sel_ref,
    uv_hbm, op_hbm, gate_hbm, up_hbm, down_hbm,
    out_ref,
    uv, op, gate, up, down, weight_sem,
    fresh_rows, lat_send, lat_recv, lat_ss, lat_rs, raised,
    shares, sh_rows,
    flat, hidden, acc, slab, blocks, total, stream, gains, squares, rows_out,
    s_send, s_recv, s_ss, s_rs,
    p_send, p_recv, p_ss, p_rs,
    z_send, z_recv, z_ss, z_rs,
    xblk, xrows, l_ss, l_rs, c_ss, c_rs, x_ss, x_rs,
):
    ep_n, sides, plane, zn, tok, hpd = dims
    n = ep_n * sides
    ep = lax.axis_index("ep")
    side = lax.axis_index("side")
    me = ep * sides + side
    z, c = ep // plane, ep % plane
    other = 1 - side
    feature = op_hbm.shape[2]
    chunks, quarters, piece = total.shape[0], total.shape[1] // tok, total.shape[2]
    tile = quarters * piece
    values = uv_hbm.shape[2]

    barrier = pltpu.get_barrier_semaphore()

    @pl.loop(1, n)
    def _(k):
        d = (me + k) % n
        pl.semaphore_signal(
            barrier, inc=1, device_id={"ep": d // sides, "side": d % sides}, device_id_type=MESH
        )

    loads = [
        pltpu.make_async_copy(uv_hbm.at[h], uv.at[:, pl.ds(h * values, values)], weight_sem.at[h])
        for h in range(hpd)
    ] + [
        pltpu.make_async_copy(op_hbm.at[0], op, weight_sem.at[hpd]),
        pltpu.make_async_copy(gate_hbm.at[0], gate, weight_sem.at[hpd + 1]),
        pltpu.make_async_copy(up_hbm.at[0], up, weight_sem.at[hpd + 2]),
        pltpu.make_async_copy(down_hbm.at[0], down, weight_sem.at[hpd + 3]),
    ]
    for load in loads:
        load.start()

    factor = 1.0 / QKD**0.5
    requests = cache_ref.shape[0]
    steps = tok // requests
    fresh_rows[...] = jnp.zeros_like(fresh_rows)
    fresh_rows[:tok, :] = fresh_ref[...].astype(F32)
    fresh = fresh_rows[...].astype(BF)
    merged_all = []
    for r in range(requests):
        q = jnp.concatenate([q_ref[r * steps + j].T for j in range(steps)], axis=0)
        keys = cache_ref[r]
        dims_t = (((1,), (1,)), ((), ()))
        s1 = jnp.dot(q, keys, preferred_element_type=F32) * factor
        s2 = lax.dot_general(q, fresh, dims_t, preferred_element_type=F32) * factor
        live1 = lax.broadcasted_iota(jnp.int32, s1.shape, 1) < lengths_ref[r]
        live2 = fresh_live_ref[r] > 0.0
        s1 = jnp.where(live1, s1, MASKED)
        s2 = jnp.where(live2, s2, MASKED)
        top = jnp.maximum(
            jnp.max(s1, axis=1, keepdims=True), jnp.max(s2, axis=1, keepdims=True)
        )
        w1 = jnp.where(live1, jnp.exp(s1 - top), 0.0)
        w2 = jnp.where(live2, jnp.exp(s2 - top), 0.0)
        weight_sum = jnp.sum(w1, axis=1, keepdims=True) + jnp.sum(w2, axis=1, keepdims=True)
        merged = lax.dot_general(
            w1.astype(BF), keys[:LAT, :], dims_t, preferred_element_type=F32
        )
        merged = merged + jnp.dot(w2.astype(BF), fresh[:, :LAT], preferred_element_type=F32)
        merged = (merged / weight_sum).astype(BF)
        ordered = jnp.dot(perm_ref[...].astype(BF), merged, preferred_element_type=F32)
        merged_all.append(ordered.reshape(n, ordered.shape[0] // n, LAT))
    lat_send[...] = jnp.concatenate(merged_all, axis=1).astype(BF)

    pl.semaphore_wait(barrier, n - 1)

    def lat_copy(d, slot):
        return remote(
            lat_send.at[d], lat_recv.at[slot], lat_ss, lat_rs.at[z], d // sides, d % sides
        )

    near, inside = me // (n // 2) * (n // 2), me % (n // 2)
    far = n // 2 - near

    @pl.loop(0, n // 2)
    def _(k):
        lat_copy(far + (inside + k * 5) % (n // 2), me).start()

    @pl.loop(1, n // 2)
    def _(k):
        lat_copy(near + (inside + k * 5) % (n // 2), me).start()

    lat_recv[me] = lat_send[me]

    lanes = lax.broadcasted_iota(jnp.int32, (tok, shares.shape[1]), 1)
    share = jnp.zeros((tok, shares.shape[1]), F32)
    for k in range(ids_ref.shape[1]):
        share = share + jnp.where(lanes == ids_ref[:, k : k + 1], weights_ref[:, k : k + 1], 0.0)
    shares[...] = jnp.zeros_like(shares)
    for a in range(3):
        term = share.astype(BF).astype(F32)
        shares[a * tok : (a + 1) * tok, :] = term
        share = share - term
    xblk[side, z, c, :, chunks * piece :] = shares[...].astype(BF)

    rows_out[...] = resid_ref[...].astype(F32)
    for j in range(chunks):
        for a in range(quarters):
            cols = slice(j * tile + a * piece, j * tile + (a + 1) * piece)
            stream[j, a * tok : (a + 1) * tok, :] = rows_out[:, cols]
            gains[j, a * tok : (a + 1) * tok, :] = jnp.broadcast_to(
                gain_ref[cols][None, :], (tok, piece)
            )

    for load in loads[: hpd + 1]:
        load.wait()

    group = plane * sides
    lat_rows = lat_recv.shape[1]

    for k in range(zn):
        layer = (z + k) % zn
        got = lat_recv.at[pl.ds(layer * group, group if k else group - 1)]
        remote(got, got, lat_ss, lat_rs.at[layer], ep, other).wait_recv()
        arrived = lat_recv[pl.ds(layer * group, group)].reshape(group * lat_rows, LAT)
        up_rows = jnp.dot(arrived, uv[...], preferred_element_type=F32).astype(BF)
        raised[layer] = up_rows * head_ref[...].astype(BF)

    everyone = raised[...].reshape(zn * group * lat_rows, raised.shape[2])
    flat[...] = jnp.dot(pick_ref[...].astype(BF), everyone, preferred_element_type=F32).astype(BF)

    cut = -(-chunks // 2)
    groups = ((0, cut), (cut, chunks - cut))

    def scatter_sum(g, value):
        def pair(i):
            part = pl.ds(*groups[i])
            return remote(
                s_send.at[g, part], s_recv.at[g, part], s_ss.at[g, i], s_rs.at[g, i], ep, other
            )

        def plane_copy(i, k):
            peer, part = (c + k) % plane, pl.ds(*groups[i])
            return remote(
                p_send.at[g, peer, part], p_recv.at[g, c, part], p_ss.at[g, i], p_rs.at[g, i],
                z * plane + peer, side,
            )

        def z_copy(i, k):
            peer, part = (z + k) % zn, pl.ds(*groups[i])
            return remote(
                z_send.at[g, peer, part], z_recv.at[g, z, part], z_ss.at[g, i], z_rs.at[g, i],
                peer * plane + c, side,
            )

        def all_plane(i):
            some, part = pl.ds(0, plane - 1), pl.ds(*groups[i])
            return remote(
                p_send.at[g, some, part], p_recv.at[g, some, part], p_ss.at[g, i], p_rs.at[g, i],
                ep, other,
            )

        def all_z(i):
            some, part = pl.ds(0, zn - 1), pl.ds(*groups[i])
            return remote(
                z_send.at[g, some, part], z_recv.at[g, some, part], z_ss.at[g, i], z_rs.at[g, i],
                ep, other,
            )

        def chunk_loop(i):
            return pl.loop(groups[i][0], groups[i][0] + groups[i][1])

        for i in range(2):

            @chunk_loop(i)
            def _(j):
                cols = pl.ds(pl.multiple_of(j * tile, tile), tile)
                acc[j] = value(cols).reshape(sides, plane, zn * tok, tile)
                s_send[g, j] = acc[j, other].astype(BF)

            pair(i).start()

        for i in range(2):
            pair(i).wait_recv()
            for k in range(1, plane):
                peer = (c + k) % plane

                @chunk_loop(i)
                def _(j):
                    p_send[g, peer, j] = (
                        acc[j, side, peer] + s_recv[g, j, peer].astype(F32)
                    ).astype(BF)

                plane_copy(i, k).start()

        for i in range(2):
            all_plane(i).wait_recv()

            @chunk_loop(i)
            def _(j):
                own = acc[j, side, c] + s_recv[g, j, c].astype(F32)
                for k in range(1, plane):
                    own = own + p_recv[g, (c + k) % plane, j].astype(F32)
                slab[...] = own
                for layer in range(zn):
                    for a in range(quarters):
                        blocks[layer, a * tok : (a + 1) * tok, :] = slab[
                            layer * tok : (layer + 1) * tok, a * piece : (a + 1) * piece
                        ]
                for layer in range(zn):
                    z_send[g, layer, j] = blocks[layer].astype(BF)
                total[j] = blocks[z]

            for k in range(1, zn):
                z_copy(i, k).start()

        for i in range(2):
            all_z(i).wait_recv()

            @chunk_loop(i)
            def _(j):
                result = total[j]
                for k in range(1, zn):
                    result = result + z_recv[g, (z + k) % zn, j].astype(F32)
                total[j] = result

        def finish():
            for i in range(2):
                pair(i).wait_send()
                all_plane(i).wait_send()
                all_z(i).wait_send()

        return finish

    def attention_part(cols):
        return jnp.dot(flat[...], op[:, cols], preferred_element_type=F32)

    finish_attention = scatter_sum(0, attention_part)
    stream[...] = stream[...] + total[...]

    square = jnp.sum(jnp.sum(stream[...] * stream[...], axis=0), axis=1, keepdims=True)
    squares[...] = jnp.broadcast_to(square, squares.shape)
    token_square = squares[:tok, :]
    for a in range(1, quarters):
        token_square = token_square + squares[a * tok : (a + 1) * tok, :]
    scale = lax.rsqrt(token_square * (1.0 / feature) + NORM_EPSILON)
    for a in range(quarters):
        squares[a * tok : (a + 1) * tok, :] = scale
    for j in range(chunks):
        xblk[side, z, c, :, j * piece : (j + 1) * piece] = (
            stream[j] * squares[...] * gains[j]
        ).astype(BF)

    def line_copy(k, slot):
        peer = (z + k) % zn
        return remote(
            xblk.at[side, z, c], xblk.at[side, slot, c], l_ss.at[peer], l_rs.at[slot],
            peer * plane + c, side,
        )

    def plane_rows(k, layer):
        return remote(
            xblk.at[side, layer, c], xblk.at[side, layer, c], c_ss.at[layer], c_rs.at[layer],
            z * plane + (c + k) % plane, side,
        )

    def plane_all(layer):
        some = xblk.at[side, layer, pl.ds(0, plane - 1)]
        return remote(some, some, c_ss.at[layer], c_rs.at[layer], ep, other)

    def pair_rows(layer, half):
        return remote(
            xblk.at[half, layer], xblk.at[half, layer], x_ss.at[layer], x_rs.at[layer], ep, other
        )

    for k in range(1, zn):
        line_copy(k, z).start()
    for k in range(1, plane):
        plane_rows(k, z).start()
    for kz in range(zn):
        layer, following = (z + kz) % zn, (z + kz + 1) % zn
        if kz + 1 < zn:
            line_copy(kz + 1, following).wait_recv()
            for k in range(1, plane):
                plane_rows(k, following).start()
        plane_all(layer).wait_recv()
        pair_rows(layer, side).start()

    for load in loads[hpd + 1 :]:
        load.wait()
    half_rows = plane * zn * tok

    def unpack(half):
        travelled = xblk[half].reshape(half_rows * quarters, xblk.shape[4])
        rows = jnp.dot(sel_ref[...].astype(BF), travelled, preferred_element_type=F32)
        for a in range(quarters):
            for j in range(chunks):
                first = j * tile + a * piece
                xrows[half, :, first : first + piece] = rows[
                    a * half_rows : (a + 1) * half_rows, j * piece : (j + 1) * piece
                ].astype(BF)
        terms = rows[:half_rows, chunks * piece :]
        for a in range(1, 3):
            terms = terms + rows[a * half_rows : (a + 1) * half_rows, chunks * piece :]
        which = lax.broadcasted_iota(jnp.int32, terms.shape, 1)
        weight = jnp.sum(jnp.where(which == ep, terms, 0.0), axis=1, keepdims=True)
        sh_rows[half] = jnp.broadcast_to(weight, sh_rows.shape[1:])

    unpack(side)
    for layer in range(zn):
        pair_rows(layer, other).wait_recv()
    unpack(other)

    units = gate.shape[1]
    step = min(units, 256)
    everything = xrows[...].reshape(sides * half_rows, feature)
    for j in range(units // step):
        cols = slice(j * step, (j + 1) * step)
        gated = jnp.dot(everything, gate[:, cols], preferred_element_type=F32)
        lifted = jnp.dot(everything, up[:, cols], preferred_element_type=F32)
        hidden[:, cols] = (gated / (1.0 + jnp.exp(-gated)) * lifted).astype(BF)

    def expert_part(cols):
        part = jnp.dot(hidden[...], down[:, cols], preferred_element_type=F32)
        weight = sh_rows[...].reshape(sides * half_rows, sh_rows.shape[2])[:, :1]
        return part.astype(BF).astype(F32) * weight

    finish_mixture = scatter_sum(1, expert_part)
    stream[...] = stream[...] + total[...]
    for j in range(chunks):
        for a in range(quarters):
            cols = slice(j * tile + a * piece, j * tile + (a + 1) * piece)
            rows_out[:, cols] = stream[j, a * tok : (a + 1) * tok, :]
    out_ref[...] = rows_out[...].astype(BF)

    finish_attention()
    finish_mixture()
    sent = lat_send.at[pl.ds(0, n - 1)]
    remote(sent, sent, lat_ss, lat_rs.at[0], ep, other).wait_send()
    for k in range(1, zn):
        line_copy(k, z).wait_send()
    for layer in range(zn):
        plane_all(layer).wait_send()
        pair_rows(layer, side).wait_send()


def local(
    queries, latent_cache, new_latent, lengths, residual, norm_gain, value_up, output_proj,
    expert_ids, expert_weights, gate_proj, up_proj, down_proj,
):
    ep_n, sides = lax.axis_size("ep"), lax.axis_size("side")
    n = ep_n * sides
    requests, context, key_width = latent_cache.shape
    tok, head_count, _ = queries.shape
    steps = tok // requests
    hpd = value_up.shape[0]
    feature = residual.shape[1]
    plane = 1
    while plane * plane < ep_n:
        plane *= 2
    zn = ep_n // plane
    quarters = 16 // tok
    piece = 128
    tile = quarters * piece
    chunks = feature // tile
    rq = -(-steps * hpd // 8) * 8
    fresh_count = 16
    lat_rows = requests * rq
    values = value_up.shape[2]
    units = gate_proj.shape[2]

    key = np.arange(fresh_count)[None, None, :]
    request = np.arange(requests)[:, None, None]
    step = (np.arange(steps * head_count) // head_count)[None, :, None]
    fresh_live = (key // steps == request) & (key % steps <= step) & (key < tok)

    perm = np.zeros((n, rq, steps * head_count), np.float32)
    for d in range(n):
        for j in range(steps):
            for h in range(hpd):
                perm[d, j * hpd + h, j * head_count + d * hpd + h] = 1.0
    perm = perm.reshape(n * rq, steps * head_count)

    pick = np.zeros((n, tok, n, lat_rows), np.float32)
    heads = np.zeros((plane * sides, lat_rows, hpd, values), np.float32)
    for d in range(n):
        e, s = d // sides, d % sides
        slot = (s * plane + e % plane) * zn + e // plane
        for t in range(tok):
            first = (t // steps) * rq + (t % steps) * hpd
            pick[slot, t, d, first : first + hpd] = 1.0
    for t in range(tok):
        for h in range(hpd):
            heads[:, (t // steps) * rq + (t % steps) * hpd + h, h] = 1.0
    pick = pick.reshape(n * tok, n * lat_rows)
    heads = heads.reshape(plane * sides * lat_rows, hpd * values)

    sel = np.zeros((quarters, plane, zn, tok, zn, plane, quarters, tok), np.float32)
    for a in range(quarters):
        for e in range(ep_n):
            for t in range(tok):
                sel[a, e % plane, e // plane, t, e // plane, e % plane, a, t] = 1.0
    sel = sel.reshape(quarters * ep_n * tok, ep_n * quarters * tok)

    lanes = -(-ep_n // 128) * 128
    op = output_proj.reshape(1, hpd * output_proj.shape[1], feature)
    half = n * tok // 2
    zr = zn * tok
    blk = quarters * tok
    dma, vm = pltpu.SemaphoreType.DMA, pltpu.VMEM
    scratch = [
        vm((LAT, hpd * values), BF), vm((hpd * values, feature), BF),
        vm((feature, units), BF), vm((feature, units), BF), vm((units, feature), BF), dma((hpd + 4,)),
        vm((fresh_count, key_width), F32),
        vm((n, lat_rows, LAT), BF), vm((n, lat_rows, LAT), BF), dma(()), dma((zn,)),
        vm((zn, plane * sides * lat_rows, hpd * values), BF),
        vm((blk, lanes), F32), vm((sides, half, lanes), F32),
        vm((2 * half, hpd * values), BF), vm((2 * half, units), BF),
        vm((chunks, sides, plane, zr, tile), F32), vm((zr, tile), F32), vm((zn, blk, piece), F32),
        vm((chunks, blk, piece), F32), vm((chunks, blk, piece), F32), vm((chunks, blk, piece), F32),
        vm((blk, piece), F32), vm((tok, feature), F32),
        vm((2, chunks, plane, zr, tile), BF), vm((2, chunks, plane, zr, tile), BF),
        dma((2, 2)), dma((2, 2)),
        vm((2, plane, chunks, zr, tile), BF), vm((2, plane, chunks, zr, tile), BF),
        dma((2, 2)), dma((2, 2)),
        vm((2, zn, chunks, blk, piece), BF), vm((2, zn, chunks, blk, piece), BF),
        dma((2, 2)), dma((2, 2)),
        vm((sides, zn, plane, blk, chunks * piece + lanes), BF), vm((sides, half, feature), BF),
        dma((zn,)), dma((zn,)), dma((zn,)), dma((zn,)), dma((zn,)), dma((zn,)),
    ]
    in_vmem = pl.BlockSpec(memory_space=pltpu.VMEM)
    in_smem = pl.BlockSpec(memory_space=pltpu.SMEM)
    in_hbm = pl.BlockSpec(memory_space=pl.ANY)
    body = functools.partial(kernel, (ep_n, sides, plane, zn, tok, hpd))
    return pl.pallas_call(
        body,
        out_shape=jax.ShapeDtypeStruct((tok, feature), BF),
        in_specs=[in_vmem] * 3 + [in_smem] + [in_vmem] * 9 + [in_hbm] * 5,
        out_specs=in_vmem,
        scratch_shapes=scratch,
        compiler_params=pltpu.CompilerParams(
            collective_id=0, has_side_effects=True, vmem_limit_bytes=60 * 2**20
        ),
    )(
        queries.transpose(0, 2, 1), latent_cache.transpose(0, 2, 1), new_latent, lengths, residual,
        norm_gain,
        expert_ids, expert_weights, jnp.asarray(fresh_live, F32), jnp.asarray(perm),
        jnp.asarray(pick), jnp.asarray(heads), jnp.asarray(sel),
        value_up, op, gate_proj, up_proj, down_proj,
    )


def solution(mesh):
    rows = ("groups", "ep", "side")
    in_specs = (
        P(rows, None, None),
        P(rows, None, None),
        P(rows, None),
        P(rows),
        P(rows, None),
        P(),
        P(("ep", "side"), None, None),
        P(("ep", "side"), None, None),
        P(rows, None),
        P(rows, None),
        P("ep", None, "side"),
        P("ep", None, "side"),
        P("ep", "side", None),
    )
    return jax.shard_map(
        local, mesh=mesh, in_specs=in_specs, out_specs=P(rows, None), check_vma=False
    )
```
